512 devices in a mesh: node: 8 (over y, z_hi), fsdp: 32 (over x, z_lo), rep: 2 (over core).
Axes of the slice: x: 4, y: 4, z: 16 (z_hi: 2, z_lo: 8; z = z_hi * 8 + z_lo), core: 2. Of those that a mesh axis runs over, the one named last changes fastest.
Arguments:
- hidden_in: bfloat16 [131072, 4096], P(('node', 'fsdp', 'rep')), may hold values from -24 to 24
- inv_rms: bfloat16 [131072], P(('node', 'fsdp', 'rep')), may hold values from 0.5 to 2
- norm_gain: float32 [4096], replicated, may hold values from 0.25 to 1.75
- key_grad: bfloat16 [131072, 512], P(('node', 'fsdp', 'rep')), may hold values from -0.015625 to 0.015625
- value_grad: bfloat16 [131072, 512], P(('node', 'fsdp', 'rep')), may hold values from -0.015625 to 0.015625
- key_weight: bfloat16 [4096, 512], P('node'), may hold values from -0.09375 to 0.09375
- value_weight: bfloat16 [4096, 512], P('node'), may hold values from -0.09375 to 0.09375
Outputs:
- key_scaled: float32 [4096, 512], P(('node', 'fsdp'))
- value_scaled: float32 [4096, 512], P(('node', 'fsdp'))
- grad_amax: float32 [2], replicated
- gain_grad: float32 [4096], replicated
The draws below stay inside these ranges and needn't reach their ends.
All inputs are finite; a program needn't handle non-finite values. Where the reference program divides by a largest or mean magnitude, that divisor is 1e-20 or more.
Results may differ from the reference program's by a relative error of at most 0.0053.
Values may be sent and summed in bfloat16 or wider, within the bound.
No kernel may reach another device: no remote copies, remote signals or barrier semaphores. Data moves between devices by JAX's collectives and lax.ppermute only.
A program may use at most 128 MiB of HBM per device.

```python
import math
import jax
import jax.numpy as jnp
from jax import lax

FEAT = 4096
KVW = 512
TOK_DEV = 256
TOKENS = 131072
N_NODE = 8
N_FSDP = 32
N_REP = 2


def raised(drawn, key, source, target, parts, factor):
    owner, partner = [(jnp.arange(drawn.shape[position]) // (drawn.shape[position] // parts)).reshape([-1 if axis == position else 1 for axis in range(drawn.ndim)]) for position in (source, target)]
    chosen = jax.random.permutation(key, parts)[partner]
    strong = (owner == chosen) | (owner == (partner + parts // 2) % parts)
    return jnp.where(strong, factor * drawn, drawn)


def block_scale(rng, shape, cuts, smallest, top_value):
    def one(dim, blocks):
        draws = jax.random.uniform(jax.random.fold_in(jax.random.fold_in(rng, 6), dim), (blocks,), jnp.float32, smallest / len(cuts), top_value / len(cuts))
        return jnp.repeat(jnp.exp(draws), shape[dim] // blocks).reshape((-1,) + (1,) * (len(shape) - dim - 1))

    factor_of = one(*cuts[0])
    for cut in cuts[1:]:
        factor_of = factor_of * one(*cut)
    return factor_of


def scatter_about(key, shape, deviation, limit, cuts=(), held_as=jnp.bfloat16):
    factor_of = block_scale(key, shape, cuts, -0.22, 0.18) if cuts else 1.0
    entries = jax.random.normal(key, shape, jnp.float32) * deviation * factor_of
    return jnp.minimum(jnp.maximum(entries, -limit), limit).astype(held_as)


def heavy_noise(own_key, extent, width, most, split, heavy, kind=jnp.bfloat16):
    entries = width * jax.random.normal(own_key, extent, jnp.float32)
    if split:
        entries = entries * block_scale(own_key, extent, split, -0.22, 0.18)
    return jnp.clip(raised(entries, jax.random.fold_in(own_key, 3), *heavy), -most, most).astype(kind)


def setup_inputs(seed: int = 0) -> dict:
    keys = jax.random.split(jax.random.key(seed), 8)
    hidden_in = heavy_noise(keys[0], (TOKENS, FEAT), 1.0, 24.0, ((0, 512),), (0, 1, 512, 6.0))
    inv_rms = jnp.clip(jnp.exp(math.log(2.0) - 1.3862944 * jax.random.uniform(keys[1], (TOKENS,), jnp.float32) ** block_scale(keys[1], (TOKENS,), ((0, 512),), -0.2, 0.2)), 0.5, 2.0).astype(jnp.bfloat16)
    norm_gain = jnp.clip(1.0 + 0.15 * jax.random.normal(keys[2], (FEAT,), jnp.float32), 0.25, 1.75)
    key_grad = scatter_about(keys[3], (TOKENS, KVW), (TOKENS ** -0.5), 0.015625, ((0, 512),))
    value_grad = scatter_about(keys[4], (TOKENS, KVW), (TOKENS ** -0.5), 0.015625, ((0, 512),))
    key_weight = scatter_about(keys[5], (FEAT, KVW), FEAT ** -0.5, 0.09375, ((0, 8),))
    value_weight = scatter_about(keys[6], (FEAT, KVW), FEAT ** -0.5, 0.09375, ((0, 8),))
    return dict(hidden_in=hidden_in, inv_rms=inv_rms, norm_gain=norm_gain, key_grad=key_grad, value_grad=value_grad, key_weight=key_weight, value_weight=value_weight)


def device_terms(index, hidden_in, inv_rms, norm_gain, both_grads, both_weights):
    begin = (index * TOK_DEV).astype(jnp.int32)
    rows_in = lax.dynamic_slice_in_dim(hidden_in, begin, TOK_DEV, 0)
    rms_in = lax.dynamic_slice_in_dim(inv_rms, begin, TOK_DEV, 0)
    grads_in = lax.dynamic_slice_in_dim(both_grads, begin, TOK_DEV, 0)
    scaled = rows_in.astype(jnp.float32) * rms_in.astype(jnp.float32)[:, None]
    normed = (scaled * norm_gain[None, :]).astype(jnp.bfloat16)
    partial_value = lax.dot_general(normed, grads_in, (((0,), (0,)), ((), ())), preferred_element_type=jnp.float32)
    partial_value = lax.optimization_barrier(partial_value.astype(jnp.bfloat16))
    back = lax.dot_general(grads_in, both_weights, (((1,), (1,)), ((), ())), preferred_element_type=jnp.float32)
    gain_term = jnp.sum(back * scaled, axis=0)
    return partial_value.astype(jnp.float32), gain_term


def reference(hidden_in, inv_rms, norm_gain, key_grad, value_grad, key_weight, value_weight):
    groups = N_FSDP * N_REP
    both_grads = jnp.concatenate([key_grad, value_grad], axis=1)
    both_weights = jnp.concatenate([key_weight, value_weight], axis=1)

    def over_groups(carry, group):
        total, gain_acc = carry

        def over_nodes(node, inner):
            node_acc, gain_inner = inner
            partial_value, gain_term = device_terms(node * groups + group, hidden_in, inv_rms, norm_gain, both_grads, both_weights)
            return node_acc + partial_value, gain_inner + gain_term

        start_acc = jnp.zeros((FEAT, 2 * KVW), jnp.float32)
        node_acc, gain_acc = lax.fori_loop(0, N_NODE, over_nodes, (start_acc, gain_acc))
        rounded = lax.optimization_barrier(node_acc.astype(jnp.bfloat16))
        return (total + rounded.astype(jnp.float32), gain_acc), None

    start = (jnp.zeros((FEAT, 2 * KVW), jnp.float32), jnp.zeros((FEAT,), jnp.float32))
    (weight_grad, gain_grad), _ = lax.scan(over_groups, start, jnp.arange(groups, dtype=jnp.int32))
    key_part = weight_grad[:, :KVW]
    value_part = weight_grad[:, KVW:]
    grad_amax = jnp.stack([jnp.max(jnp.abs(key_part)), jnp.max(jnp.abs(value_part))])
    key_scaled = key_part * (6.0 / (grad_amax[0] + 1e-6))
    value_scaled = value_part * (6.0 / (grad_amax[1] + 1e-6))
    return key_scaled, value_scaled, grad_amax, gain_grad
```

```python
import functools

import jax
import jax.numpy as jnp
import numpy as np
from jax import lax
from jax.experimental import pallas as pl
from jax.experimental.pallas import tpu as pltpu
from jax.sharding import PartitionSpec as P

ALL = ("node", "fsdp", "rep")
OWNERS = ("node", "fsdp")
NY, NZH, NX, NZL, NC = 4, 2, 4, 8, 2
INDEX = np.arange(NY * NZH * NX * NZL * NC).reshape(NY, NZH, NX, NZL, NC)
TILE = 128


def core_of(stream, y, x):
    return (stream + x + y) % 2


def plane_groups(first_axis):
    groups = []
    for zh in range(NZH):
        for zl in range(NZL):
            for stream in range(2):
                along_x = (first_axis == "x") == (stream == 0)
                for fixed in range(4):
                    members = [(fixed, x) for x in range(4)] if along_x else [(y, fixed) for y in range(4)]
                    groups.append([int(INDEX[y, zh, x, zl, core_of(stream, y, x)]) for y, x in members])
    return groups


def z_groups():
    return [
        [int(INDEX[y, z // NZL, x, z % NZL, c]) for z in range(NZH * NZL)]
        for y in range(NY) for x in range(NX) for c in range(NC)
    ]


SWAP = [(d, d ^ 1) for d in range(INDEX.size)]


def product_kernel(stream_ref, own_ref, other_ref, own_grad_ref, other_grad_ref, out_ref):
    first = pl.program_id(0)
    x_first = stream_ref[0] == 0
    for second in range(4):
        y = jnp.where(x_first, second, first)
        x = jnp.where(x_first, first, second)
        for zh in range(NZH):
            columns = pl.ds(pl.multiple_of((y * 8 + zh * 4 + x) * TILE, TILE), TILE)
            total = sum(
                lax.dot_general(
                    tokens[:, columns], grads[...], (((0,), (0,)), ((), ())), preferred_element_type=jnp.float32
                )
                for tokens, grads in ((own_ref, own_grad_ref), (other_ref, other_grad_ref))
            )
            rows = pl.ds((second * NZH + zh) * TILE, TILE)
            out_ref[0, rows, :] = total.astype(jnp.bfloat16)


def partial_product(stream, own, other, own_grad, other_grad):
    width = own_grad.shape[1]
    feats = own.shape[1]
    whole = lambda a: pl.BlockSpec(a.shape, lambda i, s: (0, 0))
    return pl.pallas_call(
        product_kernel,
        out_shape=jax.ShapeDtypeStruct((4, feats // 4, width), jnp.bfloat16),
        grid_spec=pltpu.PrefetchScalarGridSpec(
            num_scalar_prefetch=1,
            grid=(4,),
            in_specs=[whole(own), whole(other), whole(own_grad), whole(other_grad)],
            out_specs=pl.BlockSpec((1, feats // 4, width), lambda i, s: (i, 0, 0)),
        ),
        compiler_params=pltpu.CompilerParams(vmem_limit_bytes=40 * 1024 * 1024),
    )(stream, own, other, own_grad, other_grad)


def exchange_sum(parts, groups, kept):
    arrived = lax.all_to_all(parts, ALL, 0, 0, tiled=True, axis_index_groups=groups)
    return jnp.sum(arrived.astype(jnp.float32), axis=0).astype(kept)


def per_device(hidden_in, inv_rms, norm_gain, key_grad, value_grad, key_weight, value_weight):
    node, fsdp, core = lax.axis_index("node"), lax.axis_index("fsdp"), lax.axis_index("rep")
    y, x = node // NZH, fsdp // NZL
    stream = (core + x + y) % 2
    keys_here = stream == 0
    own_grad = jnp.where(keys_here, key_grad, value_grad)
    sent_grad = jnp.where(keys_here, value_grad, key_grad)
    other_grad = lax.ppermute(sent_grad, ALL, SWAP)
    scaled = hidden_in.astype(jnp.float32) * inv_rms.astype(jnp.float32)[:, None]
    normed = (scaled * norm_gain[None, :]).astype(jnp.bfloat16)
    other = lax.ppermute(normed, ALL, SWAP)
    width = key_grad.shape[1]
    parts = partial_product(stream.astype(jnp.int32).reshape(1), normed, other, own_grad, other_grad)
    line_sum = exchange_sum(parts, plane_groups("x"), jnp.bfloat16)
    plane_sum = exchange_sum(line_sum.reshape(4, -1, width), plane_groups("y"), jnp.bfloat16)
    owned = exchange_sum(plane_sum.reshape(NZH * NZL, -1, width), z_groups(), jnp.float32)
    arrived = lax.ppermute(owned, ALL, SWAP)
    key_part = jnp.where(keys_here, owned, arrived)
    value_part = jnp.where(keys_here, arrived, owned)

    rows = key_part.shape[0]
    key_rows = lax.dynamic_slice_in_dim(key_weight, fsdp * rows, rows, 0).astype(jnp.float32)
    value_rows = lax.dynamic_slice_in_dim(value_weight, fsdp * rows, rows, 0).astype(jnp.float32)
    gain_rows = lax.dynamic_slice_in_dim(norm_gain, (node * NX * NZL + fsdp) * rows, rows, 0)
    gain_local = (jnp.sum(key_part * key_rows, axis=1) + jnp.sum(value_part * value_rows, axis=1)) / gain_rows
    peaks = jnp.stack([jnp.max(jnp.abs(key_part)), jnp.max(jnp.abs(value_part))])
    told = jnp.concatenate([gain_local, peaks, jnp.zeros((TILE - rows - 2,), jnp.float32)])
    owners = lax.axis_size("node") * lax.axis_size("fsdp")
    heard = lax.all_to_all(jnp.broadcast_to(told[None, :], (owners, TILE)), OWNERS, 0, 0, tiled=True)
    gain_grad = heard[:, :rows].reshape(-1)
    grad_amax = jnp.max(heard[:, rows:rows + 2], axis=0)
    key_scaled = key_part * (6.0 / (grad_amax[0] + 1e-06))
    value_scaled = value_part * (6.0 / (grad_amax[1] + 1e-06))
    return (key_scaled, value_scaled, grad_amax, gain_grad)


def solution(mesh):
    return jax.shard_map(
        per_device,
        mesh=mesh,
        in_specs=(
            P(("node", "fsdp", "rep"), None),
            P(("node", "fsdp", "rep")),
            P(),
            P(("node", "fsdp", "rep"), None),
            P(("node", "fsdp", "rep"), None),
            P("node", None),
            P("node", None),
        ),
        out_specs=(P(("node", "fsdp"), None), P(("node", "fsdp"), None), P(), P()),
        check_vma=False,
    )
```

```python
import functools

import jax
import jax.numpy as jnp
import numpy as np
from jax import lax
from jax.experimental import pallas as pl
from jax.experimental.pallas import tpu as pltpu
from jax.sharding import PartitionSpec as P

ALL = ("node", "fsdp", "rep")
OWNERS = ("node", "fsdp")
NY, NZH, NX, NZL, NC = 4, 2, 4, 8, 2
INDEX = np.arange(NY * NZH * NX * NZL * NC).reshape(NY, NZH, NX, NZL, NC)
TILE = 128


def core_of(stream, y, x):
    return (stream + x + y) % 2


def plane_pairs(stage, offset):
    pairs = []
    for y, zh, x, zl, c in np.ndindex(*INDEX.shape):
        stream = core_of(c, y, x)
        along_x = stage == stream
        to_y, to_x = (y, (x + offset) % 4) if along_x else ((y + offset) % 4, x)
        target = INDEX[to_y, zh, to_x, zl, core_of(stream, to_y, to_x)]
        pairs.append((int(INDEX[y, zh, x, zl, c]), int(target)))
    return pairs


def z_groups():
    return [
        [int(INDEX[y, z // NZL, x, z % NZL, c]) for z in range(NZH * NZL)]
        for y in range(NY) for x in range(NX) for c in range(NC)
    ]


SWAP = [(d, d ^ 1) for d in range(INDEX.size)]


def product_kernel(width, place_ref, own_ref, other_ref, own_pack_ref, other_pack_ref, gain_ref, out_ref):
    x_first = place_ref[0] == 0
    first = place_ref[1]
    for step in range(4):
        second = lax.rem(place_ref[2] + step, 4)
        y = jnp.where(x_first, second, first)
        x = jnp.where(x_first, first, second)
        for zh in range(NZH):
            columns = pl.ds(pl.multiple_of((y * 8 + zh * 4 + x) * TILE, TILE), TILE)
            gain = gain_ref[:, columns]
            total = None
            for tokens, pack in ((own_ref, own_pack_ref), (other_ref, other_pack_ref)):
                inv_rms = pack[:, width:width + 1].astype(jnp.float32)
                normed = (tokens[:, columns].astype(jnp.float32) * inv_rms * gain).astype(jnp.bfloat16)
                term = lax.dot_general(
                    normed, pack[:, :width], (((0,), (0,)), ((), ())), preferred_element_type=jnp.float32
                )
                total = term if total is None else total + term
            rows = pl.ds((step * NZH + zh) * TILE, TILE)
            out_ref[rows, :] = total.astype(jnp.bfloat16)


def chunk_product(place, own, other, own_pack, other_pack, gain, width):
    tokens, feats = own.shape
    rows = feats // 4
    return pl.pallas_call(
        functools.partial(product_kernel, width),
        out_shape=jax.ShapeDtypeStruct((rows, width), jnp.bfloat16),
        in_specs=[pl.BlockSpec(memory_space=pltpu.SMEM)] + [pl.BlockSpec(memory_space=pltpu.VMEM)] * 5,
        out_specs=pl.BlockSpec(memory_space=pltpu.VMEM),
        cost_estimate=pl.CostEstimate(
            flops=4 * tokens * rows * width, bytes_accessed=rows * (4 * tokens + 2 * width), transcendentals=0
        ),
        compiler_params=pltpu.CompilerParams(vmem_limit_bytes=32 * 1024 * 1024),
    )(place, own, other, own_pack, other_pack, gain)


def total_of(arrays):
    total = arrays[0].astype(jnp.float32)
    for array in arrays[1:]:
        total = total + array.astype(jnp.float32)
    return total.astype(jnp.bfloat16)


def per_device(hidden_in, inv_rms, norm_gain, key_grad, value_grad, key_weight, value_weight):
    node, fsdp, core = lax.axis_index("node"), lax.axis_index("fsdp"), lax.axis_index("rep")
    y, x = node // NZH, fsdp // NZL
    stream = (core + x + y) % 2
    keys_here = stream == 0
    width = key_grad.shape[1]
    other = lax.ppermute(hidden_in, ALL, SWAP)
    inv_lanes = jnp.broadcast_to(inv_rms[:, None], (inv_rms.shape[0], TILE))
    own_pack = jnp.concatenate([jnp.where(keys_here, key_grad, value_grad), inv_lanes], axis=1)
    sent_pack = jnp.concatenate([jnp.where(keys_here, value_grad, key_grad), inv_lanes], axis=1)
    other_pack = lax.ppermute(sent_pack, ALL, SWAP)
    first = jnp.where(keys_here, x, y)
    second = jnp.where(keys_here, y, x)
    chunks = []
    for offset in (2, 1, 3, 0):
        place = jnp.stack([stream, (first + offset) % 4, second]).astype(jnp.int32)
        chunk = chunk_product(place, hidden_in, other, own_pack, other_pack, norm_gain[None, :], width)
        if offset:
            chunk = lax.ppermute(chunk, ALL, plane_pairs(0, offset))
        chunks.append(chunk.reshape(4, -1, width))
    planes = []
    for offset in (2, 1, 3, 0):
        line_sum = total_of([chunk[offset] for chunk in chunks])
        if offset:
            line_sum = lax.ppermute(line_sum, ALL, plane_pairs(1, offset))
        planes.append(line_sum)
    plane_sum = total_of(planes).reshape(NZH * NZL, -1, width)
    heard = lax.all_to_all(plane_sum, ALL, 0, 0, tiled=True, axis_index_groups=z_groups())
    owned = jnp.sum(heard.astype(jnp.float32), axis=0)
    arrived = lax.ppermute(owned, ALL, SWAP)
    key_part = jnp.where(keys_here, owned, arrived)
    value_part = jnp.where(keys_here, arrived, owned)

    rows = key_part.shape[0]
    key_rows = lax.dynamic_slice_in_dim(key_weight, fsdp * rows, rows, 0).astype(jnp.float32)
    value_rows = lax.dynamic_slice_in_dim(value_weight, fsdp * rows, rows, 0).astype(jnp.float32)
    gain_rows = lax.dynamic_slice_in_dim(norm_gain, (node * NX * NZL + fsdp) * rows, rows, 0)
    gain_local = (jnp.sum(key_part * key_rows, axis=1) + jnp.sum(value_part * value_rows, axis=1)) / gain_rows
    peaks = jnp.stack([jnp.max(jnp.abs(key_part)), jnp.max(jnp.abs(value_part))])
    told = jnp.concatenate([gain_local, peaks, jnp.zeros((TILE - rows - 2,), jnp.float32)])
    owners = lax.axis_size("node") * lax.axis_size("fsdp")
    heard = lax.all_to_all(jnp.broadcast_to(told[None, :], (owners, TILE)), OWNERS, 0, 0, tiled=True)
    gain_grad = heard[:, :rows].reshape(-1)
    grad_amax = jnp.max(heard[:, rows:rows + 2], axis=0)
    key_scaled = key_part * (6.0 / (grad_amax[0] + 1e-06))
    value_scaled = value_part * (6.0 / (grad_amax[1] + 1e-06))
    return (key_scaled, value_scaled, grad_amax, gain_grad)


def solution(mesh):
    return jax.shard_map(
        per_device,
        mesh=mesh,
        in_specs=(
            P(("node", "fsdp", "rep"), None),
            P(("node", "fsdp", "rep")),
            P(),
            P(("node", "fsdp", "rep"), None),
            P(("node", "fsdp", "rep"), None),
            P("node", None),
            P("node", None),
        ),
        out_specs=(P(("node", "fsdp"), None), P(("node", "fsdp"), None), P(), P()),
        check_vma=False,
    )
```

```python
import functools

import jax
import jax.numpy as jnp
import numpy as np
from jax import lax
from jax.experimental import pallas as pl
from jax.experimental.pallas import tpu as pltpu
from jax.sharding import PartitionSpec as P

ALL = ("node", "fsdp", "rep")
OWNERS = ("node", "fsdp")
NY, NZH, NX, NZL, NC = 4, 2, 4, 8, 2
INDEX = np.arange(NY * NZH * NX * NZL * NC).reshape(NY, NZH, NX, NZL, NC)
TILE = 128


def plane_pairs(stage, offset):
    pairs = []
    for y, zh, x, zl, c in np.ndindex(*INDEX.shape):
        along_x = stage == c
        to_y, to_x = (y, (x + offset) % 4) if along_x else ((y + offset) % 4, x)
        target = INDEX[to_y, zh, to_x, zl, c]
        pairs.append((int(INDEX[y, zh, x, zl, c]), int(target)))
    return pairs


def z_groups():
    return [
        [int(INDEX[y, z // NZL, x, z % NZL, c]) for z in range(NZH * NZL)]
        for y in range(NY) for x in range(NX) for c in range(NC)
    ]


SWAP = [(d, d ^ 1) for d in range(INDEX.size)]


def coordinates():
    node, fsdp = lax.axis_index("node"), lax.axis_index("fsdp")
    return fsdp // NZL, node // NZH, fsdp % NZL, lax.axis_index("rep") == 0


def column_kernel(key_grad_ref, value_grad_ref, own_ref, sent_ref):
    keys_here = coordinates()[3]
    own_ref[...] = jnp.where(keys_here, key_grad_ref[...], value_grad_ref[...])
    sent_ref[...] = jnp.where(keys_here, value_grad_ref[...], key_grad_ref[...])


def product_kernel(offset, own_ref, other_ref, own_grad_ref, other_grad_ref, out_ref):
    x_here, y_here, _, x_first = coordinates()
    first = lax.rem(jnp.where(x_first, x_here, y_here) + offset, 4)
    for step in range(4):
        second = lax.rem(jnp.where(x_first, y_here, x_here) + step, 4)
        y = jnp.where(x_first, second, first)
        x = jnp.where(x_first, first, second)
        for zh in range(NZH):
            columns = pl.ds(pl.multiple_of((y * 8 + zh * 4 + x) * TILE, TILE), TILE)
            total = sum(
                lax.dot_general(
                    tokens[:, columns], grads[...], (((0,), (0,)), ((), ())), preferred_element_type=jnp.float32
                )
                for tokens, grads in ((own_ref, own_grad_ref), (other_ref, other_grad_ref))
            )
            rows = pl.ds((step * NZH + zh) * TILE, TILE)
            out_ref[rows, :] = total.astype(jnp.bfloat16)


VMEM_BLOCK = pl.BlockSpec(memory_space=pltpu.VMEM)
SMEM_BLOCK = pl.BlockSpec(memory_space=pltpu.SMEM)
SMALL = pltpu.CompilerParams(vmem_limit_bytes=4 * 1024 * 1024)


def columns_of(key_grad, value_grad):
    shape = jax.ShapeDtypeStruct(key_grad.shape, key_grad.dtype)
    return pl.pallas_call(
        column_kernel,
        out_shape=(shape, shape),
        in_specs=[VMEM_BLOCK] * 2,
        out_specs=(VMEM_BLOCK, VMEM_BLOCK),
        compiler_params=SMALL,
    )(key_grad, value_grad)


def chunk_product(offset, own, other, own_grad, other_grad):
    tokens, feats = own.shape
    rows, width = feats // 4, own_grad.shape[1]
    return pl.pallas_call(
        functools.partial(product_kernel, offset),
        out_shape=jax.ShapeDtypeStruct((rows, width), jnp.bfloat16),
        in_specs=[VMEM_BLOCK] * 4,
        out_specs=VMEM_BLOCK,
        cost_estimate=pl.CostEstimate(
            flops=4 * tokens * rows * width, bytes_accessed=rows * (4 * tokens + 2 * width), transcendentals=0
        ),
        compiler_params=pltpu.CompilerParams(vmem_limit_bytes=12 * 1024 * 1024),
    )(own, other, own_grad, other_grad)


def total_of(arrays):
    total = arrays[0].astype(jnp.float32)
    for array in arrays[1:]:
        total = total + array.astype(jnp.float32)
    return total.astype(jnp.bfloat16)


def rows_of_both(owned_ref, arrived_ref):
    keys_here = coordinates()[3]
    owned, arrived = owned_ref[...], arrived_ref[...]
    return jnp.where(keys_here, owned, arrived), jnp.where(keys_here, arrived, owned)


def told_kernel(owned_ref, arrived_ref, key_weight_ref, value_weight_ref, gain_ref, told_ref):
    key_part, value_part = rows_of_both(owned_ref, arrived_ref)
    rows = key_part.shape[0]
    z_lo = coordinates()[2]
    node, fsdp = lax.axis_index("node"), lax.axis_index("fsdp")
    here = pl.ds(pl.multiple_of(fsdp * rows, rows), rows)
    products = key_part * key_weight_ref[here, :].astype(jnp.float32)
    products += value_part * value_weight_ref[here, :].astype(jnp.float32)
    gain_column = jnp.sum(products, axis=1, keepdims=True)
    lane = lax.broadcasted_iota(jnp.int32, (rows, TILE), 1)
    row = lax.broadcasted_iota(jnp.int32, (rows, TILE), 0)
    terms = jnp.sum(jnp.where(lane == z_lo * rows + row, gain_column, 0.0), axis=0, keepdims=True)
    terms = terms / gain_ref[pl.ds((node * NX * NZL + fsdp) // NZL, 1), :]
    key_peak = jnp.max(jnp.abs(key_part))
    value_peak = jnp.max(jnp.abs(value_part))
    free = jnp.where(z_lo < NZL // 2, TILE // 2, 0)
    lane = lane[:1]
    terms = jnp.where(lane == free, key_peak, terms)
    told_ref[...] = jnp.where(lane == free + 1, value_peak, terms)


def output_kernel(owned_ref, arrived_ref, heard_ref, key_scaled_ref, value_scaled_ref, amax_ref, gain_grad_ref):
    key_part, value_part = rows_of_both(owned_ref, arrived_ref)
    heard = heard_ref[...]
    lane = lax.broadcasted_iota(jnp.int32, heard.shape, 1)
    row = lax.broadcasted_iota(jnp.int32, heard.shape, 0)
    is_gain = (row % NZL < NZL // 2) == (lane < TILE // 2)
    gain_grad_ref[...] = jnp.sum(jnp.where(is_gain, heard, 0.0).reshape(-1, NZL, TILE), axis=1)
    peaks = jnp.max(jnp.where(is_gain, 0.0, heard), axis=0, keepdims=True)
    place = lane[:1] % (TILE // 2)
    for which, (part, out_ref) in enumerate(((key_part, key_scaled_ref), (value_part, value_scaled_ref))):
        peak = jnp.max(jnp.where(place == which, peaks, 0.0), axis=1, keepdims=True)
        out_ref[...] = part * (6.0 / (peak + 1e-06))
        amax_ref[which] = peak[0, 0]


def tell(owned, arrived, key_weight, value_weight, gain):
    return pl.pallas_call(
        told_kernel,
        out_shape=jax.ShapeDtypeStruct((1, TILE), jnp.float32),
        in_specs=[VMEM_BLOCK] * 5,
        out_specs=VMEM_BLOCK,
        compiler_params=SMALL,
    )(owned, arrived, key_weight, value_weight, gain)


def outputs(owned, arrived, heard):
    return pl.pallas_call(
        output_kernel,
        out_shape=(
            jax.ShapeDtypeStruct(owned.shape, jnp.float32),
            jax.ShapeDtypeStruct(owned.shape, jnp.float32),
            jax.ShapeDtypeStruct((2,), jnp.float32),
            jax.ShapeDtypeStruct((heard.shape[0] // NZL, TILE), jnp.float32),
        ),
        in_specs=[VMEM_BLOCK] * 3,
        out_specs=(VMEM_BLOCK, VMEM_BLOCK, SMEM_BLOCK, VMEM_BLOCK),
        compiler_params=SMALL,
    )(owned, arrived, heard)


def per_device(hidden_in, inv_rms, norm_gain, key_grad, value_grad, key_weight, value_weight):
    width = key_grad.shape[1]
    own_grad, sent_grad = columns_of(key_grad, value_grad)
    other_grad = lax.ppermute(sent_grad, ALL, SWAP)
    scaled = hidden_in.astype(jnp.float32) * inv_rms.astype(jnp.float32)[:, None]
    own = (scaled * norm_gain[None, :]).astype(jnp.bfloat16)
    other = lax.ppermute(own, ALL, SWAP)
    chunks = []
    for offset in (2, 1, 3, 0):
        chunk = chunk_product(offset, own, other, own_grad, other_grad)
        if offset:
            chunk = lax.ppermute(chunk, ALL, plane_pairs(0, offset))
        chunks.append(chunk.reshape(4, -1, width))
    planes = []
    for offset in (2, 1, 3, 0):
        line_sum = total_of([chunk[offset] for chunk in chunks])
        if offset:
            line_sum = lax.ppermute(line_sum, ALL, plane_pairs(1, offset))
        planes.append(line_sum)
    plane_sum = total_of(planes).reshape(NZH * NZL, -1, width)
    heard = lax.all_to_all(plane_sum, ALL, 0, 0, tiled=True, axis_index_groups=z_groups())
    owned = jnp.sum(heard.astype(jnp.float32), axis=0)
    arrived = lax.ppermute(owned, ALL, SWAP)
    told = tell(owned, arrived, key_weight, value_weight, norm_gain.reshape(-1, TILE))
    owners = lax.axis_size("node") * lax.axis_size("fsdp")
    heard = lax.all_to_all(jnp.broadcast_to(told, (owners, TILE)), OWNERS, 0, 0, tiled=True)
    key_scaled, value_scaled, grad_amax, gain_grad = outputs(owned, arrived, heard)
    return (key_scaled, value_scaled, grad_amax, gain_grad.reshape(-1))


def solution(mesh):
    return jax.shard_map(
        per_device,
        mesh=mesh,
        in_specs=(
            P(("node", "fsdp", "rep"), None),
            P(("node", "fsdp", "rep")),
            P(),
            P(("node", "fsdp", "rep"), None),
            P(("node", "fsdp", "rep"), None),
            P("node", None),
            P("node", None),
        ),
        out_specs=(P(("node", "fsdp"), None), P(("node", "fsdp"), None), P(), P()),
        check_vma=False,
    )
```

```python
import functools

import jax
import jax.numpy as jnp
import numpy as np
from jax import lax
from jax.experimental import pallas as pl
from jax.experimental.pallas import tpu as pltpu
from jax.sharding import PartitionSpec as P

ALL = ("node", "fsdp", "rep")
NY, NZH, NX, NZL, NC = 4, 2, 4, 8, 2
INDEX = np.arange(NY * NZH * NX * NZL * NC).reshape(NY, NZH, NX, NZL, NC)
TILE = 128


def plane_pairs(stage, offset):
    pairs = []
    for y, zh, x, zl, c in np.ndindex(*INDEX.shape):
        along_x = stage == c
        to_y, to_x = (y, (x + offset) % 4) if along_x else ((y + offset) % 4, x)
        target = INDEX[to_y, zh, to_x, zl, c]
        pairs.append((int(INDEX[y, zh, x, zl, c]), int(target)))
    return pairs


def z_groups():
    return [
        [int(INDEX[y, z // NZL, x, z % NZL, c]) for z in range(NZH * NZL)]
        for y in range(NY) for x in range(NX) for c in range(NC)
    ]


def level_groups():
    return [
        [int(INDEX[y, zh, x, zl, c]) for y in range(NY) for x in range(NX) for c in range(NC)]
        for zh in range(NZH) for zl in range(NZL)
    ]


SWAP = [(d, d ^ 1) for d in range(INDEX.size)]


def coordinates():
    node, fsdp = lax.axis_index("node"), lax.axis_index("fsdp")
    return fsdp // NZL, node // NZH, fsdp % NZL, lax.axis_index("rep") == 0


def column_kernel(key_grad_ref, value_grad_ref, own_ref, sent_ref):
    keys_here = coordinates()[3]
    own_ref[...] = jnp.where(keys_here, key_grad_ref[...], value_grad_ref[...])
    sent_ref[...] = jnp.where(keys_here, value_grad_ref[...], key_grad_ref[...])


def product_kernel(offset, own_ref, other_ref, own_grad_ref, other_grad_ref, out_ref):
    x_here, y_here, _, x_first = coordinates()
    first = lax.rem(jnp.where(x_first, x_here, y_here) + offset, 4)
    for step in range(4):
        second = lax.rem(jnp.where(x_first, y_here, x_here) + step, 4)
        y = jnp.where(x_first, second, first)
        x = jnp.where(x_first, first, second)
        for zh in range(NZH):
            columns = pl.ds(pl.multiple_of((y * 8 + zh * 4 + x) * TILE, TILE), TILE)
            total = sum(
                lax.dot_general(
                    tokens[:, columns], grads[...], (((0,), (0,)), ((), ())), preferred_element_type=jnp.float32
                )
                for tokens, grads in ((own_ref, own_grad_ref), (other_ref, other_grad_ref))
            )
            rows = pl.ds((step * NZH + zh) * TILE, TILE)
            out_ref[rows, :] = total.astype(jnp.bfloat16)


VMEM_BLOCK = pl.BlockSpec(memory_space=pltpu.VMEM)
SMEM_BLOCK = pl.BlockSpec(memory_space=pltpu.SMEM)
SMALL = pltpu.CompilerParams(vmem_limit_bytes=4 * 1024 * 1024)


def columns_of(key_grad, value_grad):
    shape = jax.ShapeDtypeStruct(key_grad.shape, key_grad.dtype)
    return pl.pallas_call(
        column_kernel,
        out_shape=(shape, shape),
        in_specs=[VMEM_BLOCK] * 2,
        out_specs=(VMEM_BLOCK, VMEM_BLOCK),
        compiler_params=SMALL,
    )(key_grad, value_grad)


def chunk_product(offset, own, other, own_grad, other_grad):
    tokens, feats = own.shape
    rows, width = feats // 4, own_grad.shape[1]
    return pl.pallas_call(
        functools.partial(product_kernel, offset),
        out_shape=jax.ShapeDtypeStruct((rows, width), jnp.bfloat16),
        in_specs=[VMEM_BLOCK] * 4,
        out_specs=VMEM_BLOCK,
        cost_estimate=pl.CostEstimate(
            flops=4 * tokens * rows * width, bytes_accessed=rows * (4 * tokens + 2 * width), transcendentals=0
        ),
        compiler_params=pltpu.CompilerParams(vmem_limit_bytes=12 * 1024 * 1024),
    )(own, other, own_grad, other_grad)


def total_of(arrays):
    total = arrays[0].astype(jnp.float32)
    for array in arrays[1:]:
        total = total + array.astype(jnp.float32)
    return total.astype(jnp.bfloat16)


BLOCKS = 8


def told_kernel(owned_ref, key_weight_ref, value_weight_ref, gain_ref, told_ref):
    x, y, z_lo, keys_here = coordinates()
    owned = owned_ref[...]
    rows = owned.shape[0]
    fsdp = lax.axis_index("fsdp")
    here = pl.ds(pl.multiple_of(fsdp * rows, rows), rows)
    weight = jnp.where(keys_here, key_weight_ref[here, :], value_weight_ref[here, :]).astype(jnp.float32)
    sums = jnp.sum(owned * weight, axis=1, keepdims=True)
    gain_row = gain_ref[pl.ds(lax.axis_index("node") * (NX * NZL // BLOCKS) + x, 1), :]
    lane = lax.broadcasted_iota(jnp.int32, (rows, TILE), 1)
    row = lax.broadcasted_iota(jnp.int32, (rows, TILE), 0)
    gains = jnp.sum(jnp.where(lane == z_lo * rows + row, gain_row, 0.0), axis=1, keepdims=True)
    block = lax.rem(y * NX + x + z_lo, BLOCKS)
    terms = jnp.where(lane == block * rows + row, sums / gains, 0.0)
    told_ref[0:1, :] = jnp.sum(terms, axis=0, keepdims=True)
    mine = lane[:1] == jnp.where(keys_here, 0, 1)
    told_ref[1:2, :] = jnp.where(mine, jnp.max(jnp.abs(owned)), 0.0)


def level_kernel(heard_ref, told_ref):
    heard = heard_ref[...]
    row = lax.broadcasted_iota(jnp.int32, heard.shape, 0)
    terms = jnp.where(row % 2 == 0, heard, 0.0)
    told_ref[0:2, :] = jnp.sum(terms.reshape(2, -1, TILE), axis=1)
    told_ref[2:3, :] = jnp.max(jnp.where(row % 2 == 0, 0.0, heard), axis=0, keepdims=True)
    told_ref[3:4, :] = jnp.zeros((1, TILE), jnp.float32)


def output_kernel(owned_ref, arrived_ref, heard_ref, key_scaled_ref, value_scaled_ref, amax_ref, gain_grad_ref):
    keys_here = coordinates()[3]
    owned, arrived = owned_ref[...], arrived_ref[...]
    span = TILE // BLOCKS
    heard = heard_ref[...].reshape(NZH, NZL, 4, TILE)
    lane_block = lax.broadcasted_iota(jnp.int32, heard.shape, 3) // span
    z_lo = lax.broadcasted_iota(jnp.int32, heard.shape, 1)
    for which in range(BLOCKS):
        terms = jnp.sum(jnp.where(lane_block == (which + z_lo) % BLOCKS, heard, 0.0), axis=1)
        for zh in range(NZH):
            turned = pltpu.roll(terms[zh], (TILE - which * span) % TILE, 1)
            for half in range(2):
                y, x = (half * BLOCKS + which) // NX, which % NX
                out_row = (y * NZH + zh) * NX + x
                gain_grad_ref[out_row:out_row + 1, :] = turned[half:half + 1]
    peaks = jnp.max(jnp.max(heard[:, :, 2:3, :], axis=1), axis=0)
    lane = lax.broadcasted_iota(jnp.int32, peaks.shape, 1)
    parts = ((owned, arrived, key_scaled_ref), (arrived, owned, value_scaled_ref))
    for which, (of_keys, of_values, out_ref) in enumerate(parts):
        peak = jnp.max(jnp.where(lane == which, peaks, 0.0), axis=1, keepdims=True)
        out_ref[...] = jnp.where(keys_here, of_keys, of_values) * (6.0 / (peak + 1e-06))
        amax_ref[which] = peak[0, 0]


def small_call(kernel, out_shape, out_specs, *operands):
    return pl.pallas_call(
        kernel,
        out_shape=out_shape,
        in_specs=[VMEM_BLOCK] * len(operands),
        out_specs=out_specs,
        compiler_params=SMALL,
    )(*operands)


def floats(*shape):
    return jax.ShapeDtypeStruct(shape, jnp.float32)


def told_to(groups, told):
    everyone = jnp.broadcast_to(told[None], (len(groups[0]),) + told.shape)
    heard = lax.all_to_all(everyone, ALL, 0, 0, tiled=True, axis_index_groups=groups)
    return heard.reshape(-1, TILE)


def per_device(hidden_in, inv_rms, norm_gain, key_grad, value_grad, key_weight, value_weight):
    width = key_grad.shape[1]
    own_grad, sent_grad = columns_of(key_grad, value_grad)
    other_grad = lax.ppermute(sent_grad, ALL, SWAP)
    scaled = hidden_in.astype(jnp.float32) * inv_rms.astype(jnp.float32)[:, None]
    own = (scaled * norm_gain[None, :]).astype(jnp.bfloat16)
    other = lax.ppermute(own, ALL, SWAP)
    chunks = []
    for offset in (2, 1, 3, 0):
        chunk = chunk_product(offset, own, other, own_grad, other_grad)
        if offset:
            chunk = lax.ppermute(chunk, ALL, plane_pairs(0, offset))
        chunks.append(chunk.reshape(4, -1, width))
    planes = []
    for offset in (2, 1, 3, 0):
        line_sum = total_of([chunk[offset] for chunk in chunks])
        if offset:
            line_sum = lax.ppermute(line_sum, ALL, plane_pairs(1, offset))
        planes.append(line_sum)
    plane_sum = total_of(planes).reshape(NZH * NZL, -1, width)
    heard = lax.all_to_all(plane_sum, ALL, 0, 0, tiled=True, axis_index_groups=z_groups())
    owned = jnp.sum(heard.astype(jnp.float32), axis=0)
    arrived = lax.ppermute(owned, ALL, SWAP)
    gain_rows = norm_gain.reshape(-1, TILE)
    told = small_call(told_kernel, floats(2, TILE), VMEM_BLOCK, owned, key_weight, value_weight, gain_rows)
    told = small_call(level_kernel, floats(4, TILE), VMEM_BLOCK, told_to(level_groups(), told))
    heard = told_to(z_groups(), told)
    key_scaled, value_scaled, grad_amax, gain_grad = small_call(
        output_kernel,
        (floats(*owned.shape), floats(*owned.shape), floats(2), floats(*gain_rows.shape)),
        (VMEM_BLOCK, VMEM_BLOCK, SMEM_BLOCK, VMEM_BLOCK),
        owned, arrived, heard,
    )
    return (key_scaled, value_scaled, grad_amax, gain_grad.reshape(-1))


def solution(mesh):
    return jax.shard_map(
        per_device,
        mesh=mesh,
        in_specs=(
            P(("node", "fsdp", "rep"), None),
            P(("node", "fsdp", "rep")),
            P(),
            P(("node", "fsdp", "rep"), None),
            P(("node", "fsdp", "rep"), None),
            P("node", None),
            P("node", None),
        ),
        out_specs=(P(("node", "fsdp"), None), P(("node", "fsdp"), None), P(), P()),
        check_vma=False,
    )
```

```python
import functools

import jax
import jax.numpy as jnp
import numpy as np
from jax import lax
from jax.experimental import pallas as pl
from jax.experimental.pallas import tpu as pltpu
from jax.sharding import PartitionSpec as P

ALL = ("node", "fsdp", "rep")
NY, NZH, NX, NZL, NC = 4, 2, 4, 8, 2
INDEX = np.arange(NY * NZH * NX * NZL * NC).reshape(NY, NZH, NX, NZL, NC)
TILE = 128


def plane_pairs(stage, offset):
    pairs = []
    for y, zh, x, zl, c in np.ndindex(*INDEX.shape):
        along_x = stage == c
        to_y, to_x = (y, (x + offset) % 4) if along_x else ((y + offset) % 4, x)
        target = INDEX[to_y, zh, to_x, zl, c]
        pairs.append((int(INDEX[y, zh, x, zl, c]), int(target)))
    return pairs


def z_groups():
    return [
        [int(INDEX[y, z // NZL, x, z % NZL, c]) for z in range(NZH * NZL)]
        for y in range(NY) for x in range(NX) for c in range(NC)
    ]


def level_groups():
    return [
        [int(INDEX[y, zh, x, zl, c]) for y in range(NY) for x in range(NX) for c in range(NC)]
        for zh in range(NZH) for zl in range(NZL)
    ]


SWAP = [(d, d ^ 1) for d in range(INDEX.size)]


def coordinates():
    node, fsdp = lax.axis_index("node"), lax.axis_index("fsdp")
    return fsdp // NZL, node // NZH, fsdp % NZL, lax.axis_index("rep") == 0


def column_kernel(key_grad_ref, value_grad_ref, own_ref, sent_ref):
    keys_here = coordinates()[3]
    own_ref[...] = jnp.where(keys_here, key_grad_ref[...], value_grad_ref[...])
    sent_ref[...] = jnp.where(keys_here, value_grad_ref[...], key_grad_ref[...])


def product_kernel(offset, steps, own_ref, other_ref, own_grad_ref, other_grad_ref, out_ref):
    x_here, y_here, _, x_first = coordinates()
    first = lax.rem(jnp.where(x_first, x_here, y_here) + offset, 4)
    for at, step in enumerate(steps):
        second = lax.rem(jnp.where(x_first, y_here, x_here) + step, 4)
        y = jnp.where(x_first, second, first)
        x = jnp.where(x_first, first, second)
        for zh in range(NZH):
            columns = pl.ds(pl.multiple_of((y * 8 + zh * 4 + x) * TILE, TILE), TILE)
            total = sum(
                lax.dot_general(
                    tokens[:, columns], grads[...], (((0,), (0,)), ((), ())), preferred_element_type=jnp.float32
                )
                for tokens, grads in ((own_ref, own_grad_ref), (other_ref, other_grad_ref))
            )
            rows = pl.ds((at * NZH + zh) * TILE, TILE)
            out_ref[rows, :] = total.astype(jnp.bfloat16)


VMEM_BLOCK = pl.BlockSpec(memory_space=pltpu.VMEM)
SMEM_BLOCK = pl.BlockSpec(memory_space=pltpu.SMEM)
SMALL = pltpu.CompilerParams(vmem_limit_bytes=4 * 1024 * 1024)


def columns_of(key_grad, value_grad):
    shape = jax.ShapeDtypeStruct(key_grad.shape, key_grad.dtype)
    return pl.pallas_call(
        column_kernel,
        out_shape=(shape, shape),
        in_specs=[VMEM_BLOCK] * 2,
        out_specs=(VMEM_BLOCK, VMEM_BLOCK),
        compiler_params=SMALL,
    )(key_grad, value_grad)


def chunk_product(offset, steps, own, other, own_grad, other_grad):
    tokens, feats = own.shape
    rows, width = feats // 16 * len(steps), own_grad.shape[1]
    return pl.pallas_call(
        functools.partial(product_kernel, offset, steps),
        out_shape=jax.ShapeDtypeStruct((rows, width), jnp.bfloat16),
        in_specs=[VMEM_BLOCK] * 4,
        out_specs=VMEM_BLOCK,
        cost_estimate=pl.CostEstimate(
            flops=4 * tokens * rows * width, bytes_accessed=rows * (4 * tokens + 2 * width), transcendentals=0
        ),
        compiler_params=pltpu.CompilerParams(vmem_limit_bytes=12 * 1024 * 1024),
    )(own, other, own_grad, other_grad)


def total_of(arrays):
    total = arrays[0].astype(jnp.float32)
    for array in arrays[1:]:
        total = total + array.astype(jnp.float32)
    return total


BLOCKS = 8


def told_kernel(owned_ref, key_weight_ref, value_weight_ref, gain_ref, told_ref):
    x, y, z_lo, keys_here = coordinates()
    owned = owned_ref[...]
    rows = owned.shape[0]
    fsdp = lax.axis_index("fsdp")
    here = pl.ds(pl.multiple_of(fsdp * rows, rows), rows)
    weight = jnp.where(keys_here, key_weight_ref[here, :], value_weight_ref[here, :]).astype(jnp.float32)
    sums = jnp.sum(owned * weight, axis=1, keepdims=True)
    gain_row = gain_ref[pl.ds(lax.axis_index("node") * (NX * NZL // BLOCKS) + x, 1), :]
    lane = lax.broadcasted_iota(jnp.int32, (rows, TILE), 1)
    row = lax.broadcasted_iota(jnp.int32, (rows, TILE), 0)
    gains = jnp.sum(jnp.where(lane == z_lo * rows + row, gain_row, 0.0), axis=1, keepdims=True)
    block = lax.rem(y * NX + x + z_lo, BLOCKS)
    terms = jnp.where(lane == block * rows + row, sums / gains, 0.0)
    told_ref[0:1, :] = jnp.sum(terms, axis=0, keepdims=True)
    mine = lane[:1] == jnp.where(keys_here, 0, 1)
    told_ref[1:2, :] = jnp.where(mine, jnp.max(jnp.abs(owned)), 0.0)


def level_kernel(heard_ref, told_ref):
    heard = heard_ref[...]
    row = lax.broadcasted_iota(jnp.int32, heard.shape, 0)
    terms = jnp.where(row % 2 == 0, heard, 0.0)
    told_ref[0:2, :] = jnp.sum(terms.reshape(2, -1, TILE), axis=1)
    told_ref[2:3, :] = jnp.max(jnp.where(row % 2 == 0, 0.0, heard), axis=0, keepdims=True)
    told_ref[3:4, :] = jnp.zeros((1, TILE), jnp.float32)


def output_kernel(owned_ref, arrived_ref, heard_ref, key_scaled_ref, value_scaled_ref, amax_ref, gain_grad_ref):
    keys_here = coordinates()[3]
    owned, arrived = owned_ref[...], arrived_ref[...]
    span = TILE // BLOCKS
    heard = heard_ref[...].reshape(NZH, NZL, 4, TILE)
    lane_block = lax.broadcasted_iota(jnp.int32, heard.shape, 3) // span
    z_lo = lax.broadcasted_iota(jnp.int32, heard.shape, 1)
    for which in range(BLOCKS):
        terms = jnp.sum(jnp.where(lane_block == (which + z_lo) % BLOCKS, heard, 0.0), axis=1)
        for zh in range(NZH):
            turned = pltpu.roll(terms[zh], (TILE - which * span) % TILE, 1)
            for half in range(2):
                y, x = (half * BLOCKS + which) // NX, which % NX
                out_row = (y * NZH + zh) * NX + x
                gain_grad_ref[out_row:out_row + 1, :] = turned[half:half + 1]
    peaks = jnp.max(jnp.max(heard[:, :, 2:3, :], axis=1), axis=0)
    lane = lax.broadcasted_iota(jnp.int32, peaks.shape, 1)
    parts = ((owned, arrived, key_scaled_ref), (arrived, owned, value_scaled_ref))
    for which, (of_keys, of_values, out_ref) in enumerate(parts):
        peak = jnp.max(jnp.where(lane == which, peaks, 0.0), axis=1, keepdims=True)
        out_ref[...] = jnp.where(keys_here, of_keys, of_values) * (6.0 / (peak + 1e-06))
        amax_ref[which] = peak[0, 0]


def small_call(kernel, out_shape, out_specs, *operands):
    return pl.pallas_call(
        kernel,
        out_shape=out_shape,
        in_specs=[VMEM_BLOCK] * len(operands),
        out_specs=out_specs,
        compiler_params=SMALL,
    )(*operands)


def floats(*shape):
    return jax.ShapeDtypeStruct(shape, jnp.float32)


def told_to(groups, told):
    everyone = jnp.broadcast_to(told[None], (len(groups[0]),) + told.shape)
    heard = lax.all_to_all(everyone, ALL, 0, 0, tiled=True, axis_index_groups=groups)
    return heard.reshape(-1, TILE)


def per_device(hidden_in, inv_rms, norm_gain, key_grad, value_grad, key_weight, value_weight):
    width = key_grad.shape[1]
    own_grad, sent_grad = columns_of(key_grad, value_grad)
    other_grad = lax.ppermute(sent_grad, ALL, SWAP)
    scaled = hidden_in.astype(jnp.float32) * inv_rms.astype(jnp.float32)[:, None]
    own = (scaled * norm_gain[None, :]).astype(jnp.bfloat16)
    other = lax.ppermute(own, ALL, SWAP)
    product = lambda offset, steps: chunk_product(offset, steps, own, other, own_grad, other_grad)
    passed, kept = (2, 1, 3), (0,)
    lines = {step: [] for step in passed + kept}
    for steps in (passed, kept):
        for offset in (2, 1, 3):
            chunk = lax.ppermute(product(offset, steps), ALL, plane_pairs(0, offset))
            for step, block in zip(steps, chunk.reshape(len(steps), -1, width)):
                lines[step].append(block)
    for step, block in zip(passed + kept, product(0, passed + kept).reshape(4, -1, width)):
        lines[step].append(block)
    planes = [
        lax.ppermute(total_of(lines[step]).astype(jnp.bfloat16), ALL, plane_pairs(1, step)) for step in passed
    ]
    plane_sum = total_of(lines[0] + planes).astype(jnp.bfloat16).reshape(NZH * NZL, -1, width)
    heard = lax.all_to_all(plane_sum, ALL, 0, 0, tiled=True, axis_index_groups=z_groups())
    owned = jnp.sum(heard.astype(jnp.float32), axis=0)
    arrived = lax.ppermute(owned, ALL, SWAP)
    gain_rows = norm_gain.reshape(-1, TILE)
    told = small_call(told_kernel, floats(2, TILE), VMEM_BLOCK, owned, key_weight, value_weight, gain_rows)
    told = small_call(level_kernel, floats(4, TILE), VMEM_BLOCK, told_to(level_groups(), told))
    heard = told_to(z_groups(), told)
    key_scaled, value_scaled, grad_amax, gain_grad = small_call(
        output_kernel,
        (floats(*owned.shape), floats(*owned.shape), floats(2), floats(*gain_rows.shape)),
        (VMEM_BLOCK, VMEM_BLOCK, SMEM_BLOCK, VMEM_BLOCK),
        owned, arrived, heard,
    )
    return (key_scaled, value_scaled, grad_amax, gain_grad.reshape(-1))


def solution(mesh):
    return jax.shard_map(
        per_device,
        mesh=mesh,
        in_specs=(
            P(("node", "fsdp", "rep"), None),
            P(("node", "fsdp", "rep")),
            P(),
            P(("node", "fsdp", "rep"), None),
            P(("node", "fsdp", "rep"), None),
            P("node", None),
            P("node", None),
        ),
        out_specs=(P(("node", "fsdp"), None), P(("node", "fsdp"), None), P(), P()),
        check_vma=False,
    )
```

```python
import functools

import jax
import jax.numpy as jnp
import numpy as np
from jax import lax
from jax.experimental import pallas as pl
from jax.experimental.pallas import tpu as pltpu
from jax.sharding import PartitionSpec as P

ALL = ("node", "fsdp", "rep")
NY, NZH, NX, NZL, NC = 4, 2, 4, 8, 2
INDEX = np.arange(NY * NZH * NX * NZL * NC).reshape(NY, NZH, NX, NZL, NC)
TILE = 128


def plane_pairs(stage, offset):
    pairs = []
    for y, zh, x, zl, c in np.ndindex(*INDEX.shape):
        along_x = stage == c
        to_y, to_x = (y, (x + offset) % 4) if along_x else ((y + offset) % 4, x)
        target = INDEX[to_y, zh, to_x, zl, c]
        pairs.append((int(INDEX[y, zh, x, zl, c]), int(target)))
    return pairs


def z_groups():
    return [
        [int(INDEX[y, z // NZL, x, z % NZL, c]) for z in range(NZH * NZL)]
        for y in range(NY) for x in range(NX) for c in range(NC)
    ]


def level_groups():
    return [
        [int(INDEX[y, zh, x, zl, c]) for y in range(NY) for x in range(NX) for c in range(NC)]
        for zh in range(NZH) for zl in range(NZL)
    ]


SWAP = [(d, d ^ 1) for d in range(INDEX.size)]


def coordinates():
    node, fsdp = lax.axis_index("node"), lax.axis_index("fsdp")
    return fsdp // NZL, node // NZH, fsdp % NZL, lax.axis_index("rep") == 0


def column_kernel(key_grad_ref, value_grad_ref, inv_ref, own_ref, sent_ref):
    keys_here = coordinates()[3]
    width = key_grad_ref.shape[1]
    own_ref[...] = jnp.where(keys_here, key_grad_ref[...], value_grad_ref[...])
    sent_ref[:, :width] = jnp.where(keys_here, value_grad_ref[...], key_grad_ref[...])
    sent_ref[:, width:] = jnp.broadcast_to(inv_ref[...], (inv_ref.shape[0], TILE))


def product_kernel(offset, steps, own_ref, other_ref, own_grad_ref, other_pack_ref, gain_ref, out_ref):
    x_here, y_here, _, x_first = coordinates()
    first = lax.rem(jnp.where(x_first, x_here, y_here) + offset, 4)
    for at, step in enumerate(steps):
        second = lax.rem(jnp.where(x_first, y_here, x_here) + step, 4)
        y = jnp.where(x_first, second, first)
        x = jnp.where(x_first, first, second)
        for zh in range(NZH):
            columns = pl.ds(pl.multiple_of((y * 8 + zh * 4 + x) * TILE, TILE), TILE)
            width = own_grad_ref.shape[1]
            scaled = other_ref[:, columns].astype(jnp.float32) * other_pack_ref[:, width:].astype(jnp.float32)
            other = (scaled * gain_ref[:, columns]).astype(jnp.bfloat16)
            total = sum(
                lax.dot_general(tokens, grads, (((0,), (0,)), ((), ())), preferred_element_type=jnp.float32)
                for tokens, grads in ((own_ref[:, columns], own_grad_ref[...]), (other, other_pack_ref[:, :width]))
            )
            rows = pl.ds((at * NZH + zh) * TILE, TILE)
            out_ref[rows, :] = total.astype(jnp.bfloat16)


VMEM_BLOCK = pl.BlockSpec(memory_space=pltpu.VMEM)
SMEM_BLOCK = pl.BlockSpec(memory_space=pltpu.SMEM)
SMALL = pltpu.CompilerParams(vmem_limit_bytes=4 * 1024 * 1024)


def columns_of(key_grad, value_grad, inv_column):
    tokens, width = key_grad.shape
    return pl.pallas_call(
        column_kernel,
        out_shape=(
            jax.ShapeDtypeStruct((tokens, width), key_grad.dtype),
            jax.ShapeDtypeStruct((tokens, width + TILE), key_grad.dtype),
        ),
        in_specs=[VMEM_BLOCK] * 3,
        out_specs=(VMEM_BLOCK, VMEM_BLOCK),
        compiler_params=SMALL,
    )(key_grad, value_grad, inv_column)


def chunk_product(offset, steps, own, other, own_grad, other_pack, gain):
    tokens, feats = own.shape
    rows, width = feats // 16 * len(steps), own_grad.shape[1]
    return pl.pallas_call(
        functools.partial(product_kernel, offset, steps),
        out_shape=jax.ShapeDtypeStruct((rows, width), jnp.bfloat16),
        in_specs=[VMEM_BLOCK] * 5,
        out_specs=VMEM_BLOCK,
        cost_estimate=pl.CostEstimate(
            flops=4 * tokens * rows * width, bytes_accessed=rows * (4 * tokens + 2 * width), transcendentals=0
        ),
        compiler_params=pltpu.CompilerParams(vmem_limit_bytes=12 * 1024 * 1024),
    )(own, other, own_grad, other_pack, gain)


def total_of(arrays):
    total = arrays[0].astype(jnp.float32)
    for array in arrays[1:]:
        total = total + array.astype(jnp.float32)
    return total


BLOCKS = 8


def told_kernel(owned_ref, key_weight_ref, value_weight_ref, gain_ref, told_ref):
    x, y, z_lo, keys_here = coordinates()
    owned = owned_ref[...]
    rows = owned.shape[0]
    fsdp = lax.axis_index("fsdp")
    here = pl.ds(pl.multiple_of(fsdp * rows, rows), rows)
    weight = jnp.where(keys_here, key_weight_ref[here, :], value_weight_ref[here, :]).astype(jnp.float32)
    sums = jnp.sum(owned * weight, axis=1, keepdims=True)
    gain_row = gain_ref[pl.ds(lax.axis_index("node") * (NX * NZL // BLOCKS) + x, 1), :]
    lane = lax.broadcasted_iota(jnp.int32, (rows, TILE), 1)
    row = lax.broadcasted_iota(jnp.int32, (rows, TILE), 0)
    gains = jnp.sum(jnp.where(lane == z_lo * rows + row, gain_row, 0.0), axis=1, keepdims=True)
    block = lax.rem(y * NX + x + z_lo, BLOCKS)
    terms = jnp.where(lane == block * rows + row, sums / gains, 0.0)
    told_ref[0:1, :] = jnp.sum(terms, axis=0, keepdims=True)
    mine = lane[:1] == jnp.where(keys_here, 0, 1)
    told_ref[1:2, :] = jnp.where(mine, jnp.max(jnp.abs(owned)), 0.0)


def level_kernel(heard_ref, told_ref):
    heard = heard_ref[...]
    row = lax.broadcasted_iota(jnp.int32, heard.shape, 0)
    terms = jnp.where(row % 2 == 0, heard, 0.0)
    told_ref[0:2, :] = jnp.sum(terms.reshape(2, -1, TILE), axis=1)
    told_ref[2:3, :] = jnp.max(jnp.where(row % 2 == 0, 0.0, heard), axis=0, keepdims=True)
    told_ref[3:4, :] = jnp.zeros((1, TILE), jnp.float32)


def output_kernel(owned_ref, arrived_ref, heard_ref, key_scaled_ref, value_scaled_ref, amax_ref, gain_grad_ref):
    keys_here = coordinates()[3]
    owned, arrived = owned_ref[...], arrived_ref[...]
    span = TILE // BLOCKS
    heard = heard_ref[...].reshape(NZH, NZL, 4, TILE)
    lane_block = lax.broadcasted_iota(jnp.int32, heard.shape, 3) // span
    z_lo = lax.broadcasted_iota(jnp.int32, heard.shape, 1)
    for which in range(BLOCKS):
        terms = jnp.sum(jnp.where(lane_block == (which + z_lo) % BLOCKS, heard, 0.0), axis=1)
        for zh in range(NZH):
            turned = pltpu.roll(terms[zh], (TILE - which * span) % TILE, 1)
            for half in range(2):
                y, x = (half * BLOCKS + which) // NX, which % NX
                out_row = (y * NZH + zh) * NX + x
                gain_grad_ref[out_row:out_row + 1, :] = turned[half:half + 1]
    peaks = jnp.max(jnp.max(heard[:, :, 2:3, :], axis=1), axis=0)
    lane = lax.broadcasted_iota(jnp.int32, peaks.shape, 1)
    parts = ((owned, arrived, key_scaled_ref), (arrived, owned, value_scaled_ref))
    for which, (of_keys, of_values, out_ref) in enumerate(parts):
        peak = jnp.max(jnp.where(lane == which, peaks, 0.0), axis=1, keepdims=True)
        out_ref[...] = jnp.where(keys_here, of_keys, of_values) * (6.0 / (peak + 1e-06))
        amax_ref[which] = peak[0, 0]


def small_call(kernel, out_shape, out_specs, *operands):
    return pl.pallas_call(
        kernel,
        out_shape=out_shape,
        in_specs=[VMEM_BLOCK] * len(operands),
        out_specs=out_specs,
        compiler_params=SMALL,
    )(*operands)


def floats(*shape):
    return jax.ShapeDtypeStruct(shape, jnp.float32)


def told_to(groups, told):
    everyone = jnp.broadcast_to(told[None], (len(groups[0]),) + told.shape)
    heard = lax.all_to_all(everyone, ALL, 0, 0, tiled=True, axis_index_groups=groups)
    return heard.reshape(-1, TILE)


def per_device(hidden_in, inv_rms, norm_gain, key_grad, value_grad, key_weight, value_weight):
    width = key_grad.shape[1]
    other = lax.ppermute(hidden_in, ALL, SWAP)
    inv_column = lax.optimization_barrier(inv_rms[:, None])
    own_grad, sent_pack = columns_of(key_grad, value_grad, inv_column)
    other_pack = lax.ppermute(sent_pack, ALL, SWAP)
    scaled = hidden_in.astype(jnp.float32) * inv_column.astype(jnp.float32)
    own = (scaled * norm_gain[None, :]).astype(jnp.bfloat16)
    gain = norm_gain[None, :]
    product = lambda offset, steps: chunk_product(offset, steps, own, other, own_grad, other_pack, gain)
    passed, kept = (2, 1, 3), (0,)
    lines = {step: [] for step in passed + kept}
    for steps in (passed, kept):
        for offset in (2, 1, 3):
            chunk = lax.ppermute(product(offset, steps), ALL, plane_pairs(0, offset))
            for step, block in zip(steps, chunk.reshape(len(steps), -1, width)):
                lines[step].append(block)
    for step, block in zip(passed + kept, product(0, passed + kept).reshape(4, -1, width)):
        lines[step].append(block)
    planes = [
        lax.ppermute(total_of(lines[step]).astype(jnp.bfloat16), ALL, plane_pairs(1, step)) for step in passed
    ]
    plane_sum = total_of(lines[0] + planes).astype(jnp.bfloat16).reshape(NZH * NZL, -1, width)
    heard = lax.all_to_all(plane_sum, ALL, 0, 0, tiled=True, axis_index_groups=z_groups())
    owned = jnp.sum(heard.astype(jnp.float32), axis=0)
    arrived = lax.ppermute(owned, ALL, SWAP)
    gain_rows = norm_gain.reshape(-1, TILE)
    told = small_call(told_kernel, floats(2, TILE), VMEM_BLOCK, owned, key_weight, value_weight, gain_rows)
    told = small_call(level_kernel, floats(4, TILE), VMEM_BLOCK, told_to(level_groups(), told))
    heard = told_to(z_groups(), told)
    key_scaled, value_scaled, grad_amax, gain_grad = small_call(
        output_kernel,
        (floats(*owned.shape), floats(*owned.shape), floats(2), floats(*gain_rows.shape)),
        (VMEM_BLOCK, VMEM_BLOCK, SMEM_BLOCK, VMEM_BLOCK),
        owned, arrived, heard,
    )
    return (key_scaled, value_scaled, grad_amax, gain_grad.reshape(-1))


def solution(mesh):
    return jax.shard_map(
        per_device,
        mesh=mesh,
        in_specs=(
            P(("node", "fsdp", "rep"), None),
            P(("node", "fsdp", "rep")),
            P(),
            P(("node", "fsdp", "rep"), None),
            P(("node", "fsdp", "rep"), None),
            P("node", None),
            P("node", None),
        ),
        out_specs=(P(("node", "fsdp"), None), P(("node", "fsdp"), None), P(), P()),
        check_vma=False,
    )
```

```python
import functools

import jax
import jax.numpy as jnp
import numpy as np
from jax import lax
from jax.experimental import pallas as pl
from jax.experimental.pallas import tpu as pltpu
from jax.sharding import PartitionSpec as P

ALL = ("node", "fsdp", "rep")
NY, NZH, NX, NZL, NC = 4, 2, 4, 8, 2
INDEX = np.arange(NY * NZH * NX * NZL * NC).reshape(NY, NZH, NX, NZL, NC)
TILE = 128


def plane_pairs(stage, offset):
    pairs = []
    for y, zh, x, zl, c in np.ndindex(*INDEX.shape):
        along_x = stage == c
        to_y, to_x = (y, (x + offset) % 4) if along_x else ((y + offset) % 4, x)
        target = INDEX[to_y, zh, to_x, zl, c]
        pairs.append((int(INDEX[y, zh, x, zl, c]), int(target)))
    return pairs


def z_groups():
    return [
        [int(INDEX[y, z // NZL, x, z % NZL, c]) for z in range(NZH * NZL)]
        for y in range(NY) for x in range(NX) for c in range(NC)
    ]


def level_groups():
    return [
        [int(INDEX[y, zh, x, zl, c]) for y in range(NY) for x in range(NX) for c in range(NC)]
        for zh in range(NZH) for zl in range(NZL)
    ]


SWAP = [(d, d ^ 1) for d in range(INDEX.size)]


def coordinates():
    node, fsdp = lax.axis_index("node"), lax.axis_index("fsdp")
    return fsdp // NZL, node // NZH, fsdp % NZL, lax.axis_index("rep") == 0


def column_kernel(key_grad_ref, value_grad_ref, own_ref, sent_ref):
    keys_here = coordinates()[3]
    own_ref[...] = jnp.where(keys_here, key_grad_ref[...], value_grad_ref[...])
    sent_ref[...] = jnp.where(keys_here, value_grad_ref[...], key_grad_ref[...])


def product_kernel(offset, steps, own_ref, other_ref, own_grad_ref, other_grad_ref, out_ref):
    x_here, y_here, _, x_first = coordinates()
    first = lax.rem(jnp.where(x_first, x_here, y_here) + offset, 4)
    for at, step in enumerate(steps):
        second = lax.rem(jnp.where(x_first, y_here, x_here) + step, 4)
        y = jnp.where(x_first, second, first)
        x = jnp.where(x_first, first, second)
        for zh in range(NZH):
            columns = pl.ds(pl.multiple_of((y * 8 + zh * 4 + x) * TILE, TILE), TILE)
            total = sum(
                lax.dot_general(
                    tokens[:, columns], grads[...], (((0,), (0,)), ((), ())), preferred_element_type=jnp.float32
                )
                for tokens, grads in ((own_ref, own_grad_ref), (other_ref, other_grad_ref))
            )
            rows = pl.ds((at * NZH + zh) * TILE, TILE)
            out_ref[rows, :] = total.astype(jnp.bfloat16)


VMEM_BLOCK = pl.BlockSpec(memory_space=pltpu.VMEM)
SMEM_BLOCK = pl.BlockSpec(memory_space=pltpu.SMEM)
SMALL = pltpu.CompilerParams(vmem_limit_bytes=4 * 1024 * 1024)


def columns_of(key_grad, value_grad):
    shape = jax.ShapeDtypeStruct(key_grad.shape, key_grad.dtype)
    return pl.pallas_call(
        column_kernel,
        out_shape=(shape, shape),
        in_specs=[VMEM_BLOCK] * 2,
        out_specs=(VMEM_BLOCK, VMEM_BLOCK),
        compiler_params=SMALL,
    )(key_grad, value_grad)


def chunk_product(offset, steps, own, other, own_grad, other_grad):
    tokens, feats = own.shape
    rows, width = feats // 16 * len(steps), own_grad.shape[1]
    return pl.pallas_call(
        functools.partial(product_kernel, offset, steps),
        out_shape=jax.ShapeDtypeStruct((rows, width), jnp.bfloat16),
        in_specs=[VMEM_BLOCK] * 4,
        out_specs=VMEM_BLOCK,
        cost_estimate=pl.CostEstimate(
            flops=4 * tokens * rows * width, bytes_accessed=rows * (4 * tokens + 2 * width), transcendentals=0
        ),
        compiler_params=pltpu.CompilerParams(vmem_limit_bytes=12 * 1024 * 1024),
    )(own, other, own_grad, other_grad)


def total_of(arrays):
    total = arrays[0].astype(jnp.float32)
    for array in arrays[1:]:
        total = total + array.astype(jnp.float32)
    return total


BLOCKS = 8


def told_kernel(owned_ref, key_weight_ref, value_weight_ref, gain_ref, told_ref):
    x, y, z_lo, keys_here = coordinates()
    owned = owned_ref[...]
    rows = owned.shape[0]
    fsdp = lax.axis_index("fsdp")
    here = pl.ds(pl.multiple_of(fsdp * rows, rows), rows)
    weight = jnp.where(keys_here, key_weight_ref[here, :], value_weight_ref[here, :]).astype(jnp.float32)
    sums = jnp.sum(owned * weight, axis=1, keepdims=True)
    gain_row = gain_ref[pl.ds(lax.axis_index("node") * (NX * NZL // BLOCKS) + x, 1), :]
    lane = lax.broadcasted_iota(jnp.int32, (rows, TILE), 1)
    row = lax.broadcasted_iota(jnp.int32, (rows, TILE), 0)
    gains = jnp.sum(jnp.where(lane == z_lo * rows + row, gain_row, 0.0), axis=1, keepdims=True)
    block = lax.rem(y * NX + x + z_lo, BLOCKS)
    terms = jnp.where(lane == block * rows + row, sums / gains, 0.0)
    mine = lane[:1] == jnp.where(keys_here, 0, 1)
    peak = jnp.where(mine, jnp.max(jnp.abs(owned)), 0.0)
    told = jnp.concatenate([jnp.sum(terms, axis=0, keepdims=True), peak], axis=0)
    told_ref[...] = jnp.broadcast_to(told[None], told_ref.shape)


def level_kernel(heard_ref, told_ref):
    heard = heard_ref[...]
    row = lax.broadcasted_iota(jnp.int32, heard.shape, 0)
    terms = jnp.where(row % 2 == 0, heard, 0.0)
    peaks = jnp.max(jnp.where(row % 2 == 0, 0.0, heard), axis=0, keepdims=True)
    told = jnp.concatenate([jnp.sum(terms.reshape(2, -1, TILE), axis=1), peaks, jnp.zeros_like(peaks)], axis=0)
    told_ref[...] = jnp.broadcast_to(told[None], told_ref.shape)


def output_kernel(owned_ref, arrived_ref, heard_ref, key_scaled_ref, value_scaled_ref, amax_ref, gain_grad_ref):
    keys_here = coordinates()[3]
    owned, arrived = owned_ref[...], arrived_ref[...]
    span = TILE // BLOCKS
    heard = heard_ref[...].reshape(NZH, NZL, 4, TILE)
    lane_block = lax.broadcasted_iota(jnp.int32, heard.shape, 3) // span
    z_lo = lax.broadcasted_iota(jnp.int32, heard.shape, 1)
    for which in range(BLOCKS):
        terms = jnp.sum(jnp.where(lane_block == (which + z_lo) % BLOCKS, heard, 0.0), axis=1)
        for zh in range(NZH):
            turned = pltpu.roll(terms[zh], (TILE - which * span) % TILE, 1)
            for half in range(2):
                y, x = (half * BLOCKS + which) // NX, which % NX
                out_row = (y * NZH + zh) * NX + x
                gain_grad_ref[out_row:out_row + 1, :] = turned[half:half + 1]
    peaks = jnp.max(jnp.max(heard[:, :, 2:3, :], axis=1), axis=0)
    lane = lax.broadcasted_iota(jnp.int32, peaks.shape, 1)
    parts = ((owned, arrived, key_scaled_ref), (arrived, owned, value_scaled_ref))
    for which, (of_keys, of_values, out_ref) in enumerate(parts):
        peak = jnp.max(jnp.where(lane == which, peaks, 0.0), axis=1, keepdims=True)
        out_ref[...] = jnp.where(keys_here, of_keys, of_values) * (6.0 / (peak + 1e-06))
        amax_ref[which] = peak[0, 0]


def small_call(kernel, out_shape, out_specs, *operands):
    return pl.pallas_call(
        kernel,
        out_shape=out_shape,
        in_specs=[VMEM_BLOCK] * len(operands),
        out_specs=out_specs,
        compiler_params=SMALL,
    )(*operands)


def floats(*shape):
    return jax.ShapeDtypeStruct(shape, jnp.float32)


def exchanged(groups, told):
    heard = lax.all_to_all(told, ALL, 0, 0, tiled=True, axis_index_groups=groups)
    return heard.reshape(-1, TILE)


def per_device(hidden_in, inv_rms, norm_gain, key_grad, value_grad, key_weight, value_weight):
    width = key_grad.shape[1]
    own_grad, sent_grad = columns_of(key_grad, value_grad)
    other_grad = lax.ppermute(sent_grad, ALL, SWAP)
    scaled = hidden_in.astype(jnp.float32) * inv_rms.astype(jnp.float32)[:, None]
    own = (scaled * norm_gain[None, :]).astype(jnp.bfloat16)
    other = lax.ppermute(own, ALL, SWAP)
    product = lambda offset, steps: chunk_product(offset, steps, own, other, own_grad, other_grad)
    passed, kept = (2, 1, 3), (0,)
    lines = {step: [] for step in passed + kept}
    for steps in (passed, kept):
        for offset in (2, 1, 3):
            chunk = lax.ppermute(product(offset, steps), ALL, plane_pairs(0, offset))
            for step, block in zip(steps, chunk.reshape(len(steps), -1, width)):
                lines[step].append(block)
    for step, block in zip(passed + kept, product(0, passed + kept).reshape(4, -1, width)):
        lines[step].append(block)
    planes = [
        lax.ppermute(total_of(lines[step]).astype(jnp.bfloat16), ALL, plane_pairs(1, step)) for step in passed
    ]
    plane_sum = total_of(lines[0] + planes).astype(jnp.bfloat16).reshape(NZH * NZL, -1, width)
    heard = lax.all_to_all(plane_sum, ALL, 0, 0, tiled=True, axis_index_groups=z_groups())
    owned = jnp.sum(heard.astype(jnp.float32), axis=0)
    arrived = lax.ppermute(owned, ALL, SWAP)
    gain_rows = norm_gain.reshape(-1, TILE)
    told = small_call(
        told_kernel, floats(NY * NX * NC, 2, TILE), VMEM_BLOCK, owned, key_weight, value_weight, gain_rows
    )
    told = small_call(level_kernel, floats(NZH * NZL, 4, TILE), VMEM_BLOCK, exchanged(level_groups(), told))
    heard = exchanged(z_groups(), told)
    key_scaled, value_scaled, grad_amax, gain_grad = small_call(
        output_kernel,
        (floats(*owned.shape), floats(*owned.shape), floats(2), floats(*gain_rows.shape)),
        (VMEM_BLOCK, VMEM_BLOCK, SMEM_BLOCK, VMEM_BLOCK),
        owned, arrived, heard,
    )
    return (key_scaled, value_scaled, grad_amax, gain_grad.reshape(-1))


def solution(mesh):
    return jax.shard_map(
        per_device,
        mesh=mesh,
        in_specs=(
            P(("node", "fsdp", "rep"), None),
            P(("node", "fsdp", "rep")),
            P(),
            P(("node", "fsdp", "rep"), None),
            P(("node", "fsdp", "rep"), None),
            P("node", None),
            P("node", None),
        ),
        out_specs=(P(("node", "fsdp"), None), P(("node", "fsdp"), None), P(), P()),
        check_vma=False,
    )
```
